128 devices in a mesh: fsdp: 32 (over x, z, core), sub: 4 (over y).
Axes of the slice: x: 4, y: 4, z: 4, core: 2. Of those that a mesh axis runs over, the one named last changes fastest.
Arguments:
- tokens: bfloat16 [16384, 1536], P(('fsdp', 'sub')), may hold values from -6 to 6
- cotangent: float32 [16384, 1536], P(('fsdp', 'sub')), may hold values from -6 to 6
- seq_lengths: int32 [256], replicated, may hold values from 1 to 127, as said below
- seq_owner: int32 [256], replicated, may hold values from 0 to 127, as said below
- inner_weight: float32 [2, 1536, 6144], P(None, ('fsdp', 'sub')), may hold values from -0.15625 to 0.15625
- inner_moment: float32 [2, 1536, 6144], P(None, ('fsdp', 'sub')), may hold values from -24 to 24
- inner_square: float32 [2, 1536, 6144], P(None, ('fsdp', 'sub')), may hold values from 1.4760361 to 5.9041443
- state_weight: float32 [2, 1536, 256], P(None, ('fsdp', 'sub')), may hold values from -0.15625 to 0.15625
- state_moment: float32 [2, 1536, 256], P(None, ('fsdp', 'sub')), may hold values from -24 to 24
- state_square: float32 [2, 1536, 256], P(None, ('fsdp', 'sub')), may hold values from 1.4760361 to 5.9041443
- step_weight: float32 [2, 1536, 48], P(None, ('fsdp', 'sub')), may hold values from -0.15625 to 0.15625
- step_moment: float32 [2, 1536, 48], P(None, ('fsdp', 'sub')), may hold values from -24 to 24
- step_square: float32 [2, 1536, 48], P(None, ('fsdp', 'sub')), may hold values from 1.4760361 to 5.9041443
- out_weight: float32 [2, 3072, 1536], P(None, ('fsdp', 'sub')), may hold values from -0.109375 to 0.109375
- out_moment: float32 [2, 3072, 1536], P(None, ('fsdp', 'sub')), may hold values from -40 to 40
- out_square: float32 [2, 3072, 1536], P(None, ('fsdp', 'sub')), may hold values from 4.1001 to 16.4004
- conv_weight: float32 [2, 3328, 5], P(None, ('fsdp', 'sub')), may hold values from -3 to 3
- conv_moment: float32 [2, 3328, 5], P(None, ('fsdp', 'sub')), may hold values from -40 to 40
- conv_square: float32 [2, 3328, 5], P(None, ('fsdp', 'sub')), may hold values from 4.1001 to 16.4004
- gains: float32 [2, 4608], P(None, ('fsdp', 'sub')), may hold values from 0.5 to 1.5
- gain_moment: float32 [2, 4608], P(None, ('fsdp', 'sub')), may hold values from -40 to 40
- gain_square: float32 [2, 4608], P(None, ('fsdp', 'sub')), may hold values from 4.1001 to 16.4004
- head_params: float32 [2, 3, 48], P(None, None, 'sub')
- head_moment: float32 [2, 3, 48], P(None, None, 'sub'), may hold values from -192 to 192
- head_square: float32 [2, 3, 48], P(None, None, 'sub'), may hold values from 94.46631 to 377.86523
Outputs:
- activations: float32 [16384, 1536], P(('fsdp', 'sub'))
- input_grad: float32 [16384, 1536], P(('fsdp', 'sub'))
- new_inner_weight: float32 [2, 1536, 6144], P(None, ('fsdp', 'sub'))
- new_inner_moment: float32 [2, 1536, 6144], P(None, ('fsdp', 'sub'))
- new_inner_square: float32 [2, 1536, 6144], P(None, ('fsdp', 'sub'))
- new_state_weight: float32 [2, 1536, 256], P(None, ('fsdp', 'sub'))
- new_state_moment: float32 [2, 1536, 256], P(None, ('fsdp', 'sub'))
- new_state_square: float32 [2, 1536, 256], P(None, ('fsdp', 'sub'))
- new_step_weight: float32 [2, 1536, 48], P(None, ('fsdp', 'sub'))
- new_step_moment: float32 [2, 1536, 48], P(None, ('fsdp', 'sub'))
- new_step_square: float32 [2, 1536, 48], P(None, ('fsdp', 'sub'))
- new_out_weight: float32 [2, 3072, 1536], P(None, ('fsdp', 'sub'))
- new_out_moment: float32 [2, 3072, 1536], P(None, ('fsdp', 'sub'))
- new_out_square: float32 [2, 3072, 1536], P(None, ('fsdp', 'sub'))
- new_conv_weight: float32 [2, 3328, 5], P(None, ('fsdp', 'sub'))
- new_conv_moment: float32 [2, 3328, 5], P(None, ('fsdp', 'sub'))
- new_conv_square: float32 [2, 3328, 5], P(None, ('fsdp', 'sub'))
- new_gains: float32 [2, 4608], P(None, ('fsdp', 'sub'))
- new_gain_moment: float32 [2, 4608], P(None, ('fsdp', 'sub'))
- new_gain_square: float32 [2, 4608], P(None, ('fsdp', 'sub'))
- new_head_params: float32 [2, 3, 48], P(None, None, 'sub')
- new_head_moment: float32 [2, 3, 48], P(None, None, 'sub')
- new_head_square: float32 [2, 3, 48], P(None, None, 'sub')
- grad_inner: float32 [2, 1536, 6144], P(None, ('fsdp', 'sub'))
- grad_state: float32 [2, 1536, 256], P(None, ('fsdp', 'sub'))
- grad_step: float32 [2, 1536, 48], P(None, ('fsdp', 'sub'))
- grad_out: float32 [2, 3072, 1536], P(None, ('fsdp', 'sub'))
- grad_conv: float32 [2, 3328, 5], P(None, ('fsdp', 'sub'))
- grad_gains: float32 [2, 4608], P(None, ('fsdp', 'sub'))
- grad_head: float32 [2, 3, 48], P(None, None, 'sub')
The draws below stay inside these ranges and needn't reach their ends.
Inputs may be any that keep to these rules, and one draw needn't show every extreme that they name: `seq_lengths`: each device owns exactly two sequences; the two sequences of one device hold 64 to 128 tokens together, exactly 128 on some device in every draw, and lengths 1 and 127 occur in every draw. `seq_owner`: every device index appears exactly twice.
All inputs are finite; a program needn't handle non-finite values.
Results may differ from the reference program's by a relative error of at most 0.02.
The reference program's roundings to bfloat16 on the way count: a program that leaves them out, or rounds other values in their place, can miss the bound.
Values may be sent and summed in bfloat16 or wider, within the bound.
A program may use at most 512 MiB of HBM per device.

```python
import math
import jax
import jax.numpy as jnp
from jax import lax

D = 1536
H = 48
P_SIZE = 64
N = 128
CONV = 4
LAYERS = 2
STEP = 10
CAP = 128
DI = 3072
CC = 3328
TOKENS = 16384
N_FSDP = 32
N_SUB = 4


def seq_plan(key):
    devices = N_FSDP * N_SUB
    key_load, key_full, key_split, key_order = jax.random.split(key, 4)
    load = jax.random.randint(key_load, (devices,), CAP // 2, CAP + 1)
    fullest = jax.random.randint(key_full, (), 0, devices)
    is_full = jnp.arange(devices) == fullest
    load = jnp.where(is_full, CAP, load)
    length_one = jax.random.randint(key_split, (devices,), 1, load)
    length_one = jnp.where(is_full, 1, length_one)
    slot_length = jnp.stack([length_one, load - length_one], axis=1).reshape(-1)
    order = jax.random.permutation(key_order, 2 * devices)
    return (slot_length[order].astype(jnp.int32), (order // 2).astype(jnp.int32))


def draw_seq_lengths(key, part):
    lengths, owners = seq_plan(key)
    return lengths


def draw_seq_owner(key, part):
    lengths, owners = seq_plan(key)
    return owners


def draw_head_params(key, part):
    key = jax.random.fold_in(key, 11)
    key_bias, key_rate, key_skip = jax.random.split(key, 3)
    bias = jax.random.uniform(key_bias, (LAYERS, H), jnp.float32, -5.0, -3.0)
    rate = jax.random.uniform(key_rate, (LAYERS, H), jnp.float32, -3.0, 0.69)
    skip = jax.random.uniform(key_skip, (LAYERS, H), jnp.float32, 0.5, 1.5)
    return jnp.stack([bias, rate, skip], axis=1)


def shard_levels(stream_key, shape, shards, low, largest):
    level, own = 1.0, jax.random.fold_in(stream_key, 6)
    for dim, parts in shards:
        heights = jnp.exp(jax.random.uniform(jax.random.fold_in(own, dim), (parts,), jnp.float32, low / len(shards), largest / len(shards)))
        level = level * jnp.repeat(heights, shape[dim] // parts).reshape([-1 if axis == dim else 1 for axis in range(len(shape))])
    return level


def normal_values(own_key, extent, scale, most, pieces=(), kind=jnp.bfloat16):
    array = scale * jax.random.normal(own_key, extent, jnp.float32)
    if pieces:
        array = array * shard_levels(own_key, extent, pieces, -0.22, 0.18)
    return jnp.clip(array, -most, most).astype(kind)


def setup_inputs(seed: int = 0) -> dict:
    key_list = jax.random.split(jax.random.key(seed), 26)
    return {
        "tokens": normal_values(key_list[0], (TOKENS, D), 1.0, 6.0, ((0, 128),)),
        "cotangent": normal_values(key_list[1], (TOKENS, D), 1.0, 6.0, ((0, 128),), jnp.float32),
        "seq_lengths": draw_seq_lengths(jax.random.fold_in(key_list[25], 71), 0),
        "seq_owner": draw_seq_owner(jax.random.fold_in(key_list[25], 71), 0),
        "inner_weight": normal_values(key_list[4], (LAYERS, D, 2 * DI), D ** -0.5, 0.15625, ((1, 128),), jnp.float32),
        "inner_moment": normal_values(key_list[5], (LAYERS, D, 2 * DI), (0.3 * TOKENS ** 0.5 / 9), 24.0, ((1, 128),), jnp.float32),
        "inner_square": jnp.clip(jnp.exp(math.log(5.9041443) - 1.3862944 * jax.random.uniform(key_list[6], (LAYERS, D, 2 * DI), jnp.float32) ** shard_levels(key_list[6], (LAYERS, D, 2 * DI), ((1, 128),), -0.2, 0.2)), 1.4760361, 5.9041443),
        "state_weight": normal_values(key_list[7], (LAYERS, D, 2 * N), D ** -0.5, 0.15625, ((1, 128),), jnp.float32),
        "state_moment": normal_values(key_list[8], (LAYERS, D, 2 * N), (0.3 * TOKENS ** 0.5 / 9), 24.0, ((1, 128),), jnp.float32),
        "state_square": jnp.clip(jnp.exp(math.log(5.9041443) - 1.3862944 * jax.random.uniform(key_list[9], (LAYERS, D, 2 * N), jnp.float32) ** shard_levels(key_list[9], (LAYERS, D, 2 * N), ((1, 128),), -0.2, 0.2)), 1.4760361, 5.9041443),
        "step_weight": normal_values(key_list[10], (LAYERS, D, H), D ** -0.5, 0.15625, ((1, 128),), jnp.float32),
        "step_moment": normal_values(key_list[11], (LAYERS, D, H), (0.3 * TOKENS ** 0.5 / 9), 24.0, ((1, 128),), jnp.float32),
        "step_square": jnp.clip(jnp.exp(math.log(5.9041443) - 1.3862944 * jax.random.uniform(key_list[12], (LAYERS, D, H), jnp.float32) ** shard_levels(key_list[12], (LAYERS, D, H), ((1, 128),), -0.2, 0.2)), 1.4760361, 5.9041443),
        "out_weight": normal_values(key_list[13], (LAYERS, DI, D), DI ** -0.5, 0.109375, ((1, 128),), jnp.float32),
        "out_moment": normal_values(key_list[14], (LAYERS, DI, D), (0.5 * TOKENS ** 0.5 / 9), 40.0, ((1, 128),), jnp.float32),
        "out_square": jnp.clip(jnp.exp(math.log(16.4004) - 1.3862944 * jax.random.uniform(key_list[15], (LAYERS, DI, D), jnp.float32) ** shard_levels(key_list[15], (LAYERS, DI, D), ((1, 128),), -0.2, 0.2)), 4.1001, 16.4004),
        "conv_weight": normal_values(key_list[16], (LAYERS, CC, CONV + 1), 0.5, 3.0, ((1, 128),), jnp.float32),
        "conv_moment": normal_values(key_list[17], (LAYERS, CC, CONV + 1), (0.5 * TOKENS ** 0.5 / 9), 40.0, ((1, 128),), jnp.float32),
        "conv_square": jnp.clip(jnp.exp(math.log(16.4004) - 1.3862944 * jax.random.uniform(key_list[18], (LAYERS, CC, CONV + 1), jnp.float32) ** shard_levels(key_list[18], (LAYERS, CC, CONV + 1), ((1, 128),), -0.2, 0.2)), 4.1001, 16.4004),
        "gains": jnp.clip(1.0 + 0.1 * jax.random.normal(key_list[19], (LAYERS, D + DI), jnp.float32), 0.5, 1.5),
        "gain_moment": normal_values(key_list[20], (LAYERS, D + DI), (0.5 * TOKENS ** 0.5 / 9), 40.0, ((1, 128),), jnp.float32),
        "gain_square": jnp.clip(jnp.exp(math.log(16.4004) - 1.3862944 * jax.random.uniform(key_list[21], (LAYERS, D + DI), jnp.float32) ** shard_levels(key_list[21], (LAYERS, D + DI), ((1, 128),), -0.2, 0.2)), 4.1001, 16.4004),
        "head_params": draw_head_params(jax.random.fold_in(key_list[25], 71), 0),
        "head_moment": normal_values(key_list[23], (LAYERS, 3, H), (0.3 * (TOKENS * P_SIZE) ** 0.5 / 9), 192.0, ((2, 4),), jnp.float32),
        "head_square": jnp.clip(jnp.exp(math.log(377.86523) - 1.3862944 * jax.random.uniform(key_list[24], (LAYERS, 3, H), jnp.float32) ** shard_levels(key_list[24], (LAYERS, 3, H), ((2, 4),), -0.2, 0.2)), 94.46631, 377.86523),
    }


EPS_NORM = 1e-05
BETA_ONE = 0.9
BETA_TWO = 0.999
ADAM_EPS = 1e-08
RATE_MATRIX = 0.05
RATE_VECTOR = 0.5
RATE_HEADS = 2.0
WEIGHT_DECAY = 0.1
HIGH = lax.Precision.HIGHEST

@jax.custom_vjp
def low(v):
    return lax.optimization_barrier(v.astype(jnp.bfloat16)).astype(jnp.float32)

@jax.custom_vjp
def low_back(v):
    return v

def low_keep(v):
    return (low(v), None)

def low_pass(kept, grad):
    return (grad,)

def back_keep(v):
    return (v, None)

def back_low(kept, grad):
    return (low(grad),)
low.defvjp(low_keep, low_pass)
low_back.defvjp(back_keep, back_low)

def seq_layout(seq_lengths, seq_owner, device, slots):
    owned = (seq_owner == device).astype(jnp.int32)
    before = jnp.cumsum(owned) - owned
    length_one = jnp.sum(seq_lengths * owned * (before == 0).astype(jnp.int32))
    length_two = jnp.sum(seq_lengths * owned * (before == 1).astype(jnp.int32))
    place = jnp.arange(slots, dtype=jnp.int32)
    segment = jnp.where(place < length_one, 0, jnp.where(place < length_one + length_two, 1, 2)).astype(jnp.int32)
    live = (place < length_one + length_two).astype(jnp.float32)
    return (segment, live)

def rms_scale(values, gain):
    return values * lax.rsqrt(lax.optimization_barrier(jnp.mean(values * values, axis=1, keepdims=True)) + EPS_NORM) * gain

def prepare(proj_zx, proj_bc, proj_dt, conv_par, head_layer, segment):
    slots = proj_zx.shape[0]
    inner_width = proj_zx.shape[1] // 2
    state = proj_bc.shape[1] // 2
    nheads = head_layer.shape[1]
    head_size = inner_width // nheads
    taps = conv_par.shape[1] - 1
    conv_in = jnp.concatenate([proj_zx[:, inner_width:], proj_bc], axis=1)
    conved = conv_par[:, taps] + jnp.zeros_like(conv_in)
    for lag in range(taps):
        moved = jnp.pad(conv_in, ((lag, 0), (0, 0)))[:slots]
        earlier = jnp.pad(segment, (lag, 0), constant_values=-1)[:slots]
        same = (earlier == segment).astype(jnp.float32)[:, None]
        conved = conved + conv_par[:, taps - 1 - lag] * moved * same
    active = jax.nn.silu(conved)
    values = active[:, :inner_width]
    state_in = active[:, inner_width:inner_width + state]
    state_out = active[:, inner_width + state:]
    step_size = jax.nn.softplus(proj_dt + head_layer[0])
    level = jnp.cumsum(step_size * -jnp.exp(head_layer[1]), axis=0)
    place = jnp.arange(slots)
    allowed = ((place[:, None] >= place[None, :]) & (segment[:, None] == segment[None, :]))[None]
    gap = level.T[:, :, None] - level.T[:, None, :]
    decay = jnp.where(allowed, jnp.exp(jnp.where(allowed, gap, 0.0)), 0.0)
    scaled = values.reshape(slots, nheads, head_size) * step_size[:, :, None]
    skip_term = values * jnp.repeat(head_layer[2], head_size)
    z_gate = jax.nn.silu(proj_zx[:, :inner_width])
    return (state_in, state_out, scaled, decay, skip_term, z_gate)

def finish(ssd_out, skip_term, z_gate, gate_gain):
    return rms_scale((ssd_out + skip_term) * z_gate, gate_gain)

def mixer_layer(resid, segment, live, weights, head_layer):
    inner_w, state_w, step_w, out_w, conv_w, gain_w = weights
    width = resid.shape[1]
    normed = low(rms_scale(resid, gain_w[:width])) * live[:, None]
    proj_zx = low_back(jnp.dot(normed, inner_w, precision=HIGH))
    proj_bc = low_back(jnp.dot(normed, state_w, precision=HIGH))
    proj_dt = low_back(jnp.dot(normed, step_w, precision=HIGH))
    state_in, state_out, scaled, decay, skip_term, z_gate = prepare(proj_zx, proj_bc, proj_dt, conv_w, head_layer, segment)
    inner = low_back(jnp.dot(low(state_out), low(state_in).T, precision=HIGH))
    mixed = jnp.einsum('hts,shp->thp', low(inner[None] * decay), low(scaled), precision=HIGH)
    ssd_out = low_back(mixed).reshape(resid.shape[0], -1)
    normed_gate = finish(ssd_out, skip_term, z_gate, gain_w[width:])
    branch = low_back(jnp.dot(low(normed_gate), out_w, precision=HIGH))
    return resid + live[:, None] * branch

def adam(weight, moment, square, grad, rate, decay):
    moment = BETA_ONE * moment + (1.0 - BETA_ONE) * grad
    square = BETA_TWO * square + (1.0 - BETA_TWO) * grad * grad
    corr_one = 1.0 - BETA_ONE ** STEP
    corr_two = 1.0 - BETA_TWO ** STEP
    weight = weight - rate * (moment / corr_one / (jnp.sqrt(square / corr_two) + ADAM_EPS) + decay * weight)
    return (weight, moment, square)

def reference(tokens, cotangent, seq_lengths, seq_owner, inner_weight, inner_moment, inner_square, state_weight, state_moment, state_square, step_weight, step_moment, step_square, out_weight, out_moment, out_square, conv_weight, conv_moment, conv_square, gains, gain_moment, gain_square, head_params, head_moment, head_square):
    devices = N_FSDP * N_SUB
    group = min(8, devices)

    def forward(params, stream):
        low_params = tuple((low(param) for param in params[:6]))
        head_all = params[6]
        blocks = stream.reshape(devices // group, group, CAP, D)
        owners = jnp.arange(devices, dtype=jnp.int32).reshape(devices // group, group)

        def one_device(block, device):
            segment, live = seq_layout(seq_lengths, seq_owner, device, CAP)
            resid = block
            for layer in range(LAYERS):
                resid = mixer_layer(resid, segment, live, tuple((param[layer] for param in low_params)), head_all[layer])
            return resid

        def run_group(carry, item):
            return (carry, jax.vmap(one_device)(item[0], item[1]))
        _, result = lax.scan(jax.checkpoint(run_group), jnp.zeros((), jnp.float32), (blocks, owners))
        return result.reshape(devices * CAP, D)
    params = (inner_weight, state_weight, step_weight, out_weight, conv_weight, gains, head_params)
    activations, pullback = jax.vjp(forward, params, tokens.astype(jnp.float32))
    grads, input_grad = pullback(cotangent)
    inner_new, inner_m, inner_v = adam(inner_weight, inner_moment, inner_square, grads[0], RATE_MATRIX, WEIGHT_DECAY)
    state_new, state_m, state_v = adam(state_weight, state_moment, state_square, grads[1], RATE_MATRIX, WEIGHT_DECAY)
    step_new, step_m, step_v = adam(step_weight, step_moment, step_square, grads[2], RATE_MATRIX, WEIGHT_DECAY)
    out_new, out_m, out_v = adam(out_weight, out_moment, out_square, grads[3], RATE_MATRIX, WEIGHT_DECAY)
    conv_new, conv_m, conv_v = adam(conv_weight, conv_moment, conv_square, grads[4], RATE_VECTOR, 0.0)
    gain_new, gain_m, gain_v = adam(gains, gain_moment, gain_square, grads[5], RATE_VECTOR, 0.0)
    head_new, head_m, head_v = adam(head_params, head_moment, head_square, grads[6], RATE_HEADS, 0.0)
    return (activations, input_grad, inner_new, inner_m, inner_v, state_new, state_m, state_v, step_new, step_m, step_v, out_new, out_m, out_v, conv_new, conv_m, conv_v, gain_new, gain_m, gain_v, head_new, head_m, head_v, grads[0], grads[1], grads[2], grads[3], grads[4], grads[5], grads[6])
```

```python
from functools import partial

import jax
import jax.numpy as jnp
import numpy as np
from jax import lax
from jax.experimental import pallas as pl
from jax.experimental.pallas import tpu as pltpu
from jax.sharding import PartitionSpec as P

STEP = 10

EPS_NORM = 1e-05
BETA_ONE = 0.9
BETA_TWO = 0.999
ADAM_EPS = 1e-08
RATE_MATRIX = 0.05
RATE_VECTOR = 0.5
RATE_HEADS = 2.0
WEIGHT_DECAY = 0.1

MESH = pl.DeviceIdType.MESH
BF = jnp.bfloat16
F32 = jnp.float32
ANY = pl.BlockSpec(memory_space=pl.ANY)
VMEM = pl.BlockSpec(memory_space=pltpu.VMEM)

WIDTH = 1536
INNER = 3072
STATE = 128
HEADS = 48
LAYERS = 2
WA = 3584
WIN = WA + INNER
PARTS = (
    ("in", 0, 2560, "x"),
    ("in", 2560, 2048, "z"),
    ("in", 4608, 2048, "y"),
    ("out", 0, 512, "x"),
    ("out", 512, 512, "z"),
    ("out", 1024, 512, "y"),
)
BLOCK_ROWS = {"in": 48, "out": 96}
PADDED = {"in": 16, "out": 32}
MATRIX = {"in": (4, 4, 2, 48, WIN), "out": (4, 4, 2, 96, WIDTH)}


def place():
    f = lax.axis_index("fsdp")
    y = lax.axis_index("sub")
    return lax.div(f, 8), lax.rem(lax.div(f, 2), 4), lax.rem(f, 2), y


def device_at(x, z, core, y):
    return (x * 8 + z * 2 + core, y)


def turn(i, by):
    return lax.rem(i + by, 4)


class Wire:
    def __init__(self, send, recv):
        self.send, self.recv, self.copies, self.left_source = send, recv, [], []
        self.x, self.z, self.core, self.y = place()
        x, z, c, y = self.x, self.z, self.core, self.y
        self.partner = device_at(x, z, 1 - c, y)
        self.right = {
            "x": device_at(turn(x, 1), z, c, y),
            "z": device_at(x, turn(z, 1), c, y),
            "y": device_at(x, z, c, turn(y, 1)),
        }
        self.left = {
            "x": device_at(turn(x, 3), z, c, y),
            "z": device_at(x, turn(z, 3), c, y),
            "y": device_at(x, z, c, turn(y, 3)),
        }
        self.index = {"x": x, "z": z, "y": y}

    def greet(self):
        barrier = pltpu.get_barrier_semaphore()
        x, z, c, y = self.x, self.z, self.core, self.y
        peers = [self.partner, device_at(x, z, c, turn(y, 2))]
        peers += list(self.right.values()) + list(self.left.values())
        for peer in peers:
            pl.semaphore_signal(barrier, inc=1, device_id=peer, device_id_type=MESH)
        pl.semaphore_wait(barrier, len(peers))

    def copy(self, src, dst, device):
        number = len(self.copies)
        made = pltpu.make_async_remote_copy(
            src_ref=src,
            dst_ref=dst,
            send_sem=self.send.at[number],
            recv_sem=self.recv.at[number],
            device_id=device,
            device_id_type=MESH,
        )
        made.start()
        self.copies.append(made)
        return made

    def sent(self, made):
        made.wait_send()
        self.left_source.append(made)

    def finish(self):
        for made in self.copies:
            if not any(made is other for other in self.left_source):
                made.wait_send()


def cols(base, j, width, start=0, size=None):
    return pl.ds(pl.multiple_of(base + j * width + start, 128), width if size is None else size)


def dot(left, right):
    return jnp.dot(left, right, preferred_element_type=F32)


def block_half(rows, width):
    if width >= 256:
        first = width // 256 * 128

        def cut(h):
            return (0, rows), {None: (0, width), 0: (0, first), 1: (first, width - first)}[h]
    else:
        first = rows // 32 * 16 if rows % 32 == 0 else rows // 3 * 2

        def cut(h):
            return {None: (0, rows), 0: (0, first), 1: (first, rows - first)}[h], (0, width)
    return cut


def picker(block, pad):
    rows = 4 * block
    pick = np.zeros((rows, 4 * pad), np.float32)
    for r in range(rows):
        pick[r, (r // block) * pad + r % block] = 1.0
    return pick


def gather_regions(part, out, x, z, c, y):
    if part is None:
        half = lambda h: pl.ds(0, 4) if h is None else pl.ds(2 * h, 2)
        one = lambda j, h: None if h == 1 else out.at[x, z, c, j]
        two = lambda j, h: out.at[x, j, c, half(h)]
        three = lambda j, h: out.at[half(h), j, c]
        return (("y", one), ("z", two), ("x", lambda j, h: out.at[j, half(h), c]))
    kind, base, width, last = part
    quarter = width // 4
    half = lambda h: pl.ds(0, 4) if h is None else pl.ds(2 * h, 2)
    full = pl.ds(base, width)
    cut = block_half(BLOCK_ROWS[kind], quarter)

    def block(h, q):
        (row, rows), (col, size) = cut(h)
        return pl.ds(row, rows), cols(base, q, quarter, col, size)

    if last == "x":

        def one(j, h):
            at = block(h, j)
            return out.at[x, z, c, at[0], at[1]]

        def two(j, h):
            size = width if h is None else width // 2
            return out.at[x, j, c, :, pl.ds(base + (h or 0) * size, size)]

        return (("y", one), ("z", two), ("x", lambda j, h: out.at[j, half(h), c, :, full]))
    if last == "z":

        def one(j, h):
            at = block(h, y)
            return out.at[j, z, c, at[0], at[1]]

        two = lambda j, h: out.at[half(h), z, c, :, cols(base, j, quarter)]
        return (("x", one), ("y", two), ("z", lambda j, h: out.at[half(h), j, c, :, full]))

    def one(j, h):
        at = block(h, y)
        return out.at[x, j, c, at[0], at[1]]

    two = lambda j, h: out.at[j, half(h), c, :, cols(base, y, quarter)]
    return (("z", one), ("x", two), ("y", lambda j, h: out.at[half(h), :, c, :, cols(base, j, quarter)]))


class Gather:
    def __init__(self, wire, plans):
        self.wire, self.plans, self.partner = wire, plans, []

    def forward(self, ref):
        self.partner.append(self.wire.copy(ref, ref, self.wire.partner))

    def start(self, phase):
        wire, self.nears = self.wire, []
        for plan in self.plans:
            axis, region = plan[phase]
            own = region(wire.index[axis], None)
            self.nears.append((wire.copy(own, own, wire.right[axis]), wire.copy(own, own, wire.left[axis])))
        if phase == 2:
            for plan in self.plans:
                axis, region = plan[phase]
                self.forward(region(wire.index[axis], None))

    def middle(self, phase):
        wire, self.fars = self.wire, []
        for plan, (to_right, to_left) in zip(self.plans, self.nears):
            axis, region = plan[phase]
            i = wire.index[axis]
            sent = []
            to_right.wait_recv()
            ref = region(turn(i, 3), 0)
            sent.append(wire.copy(ref, ref, wire.right[axis]))
            to_left.wait_recv()
            ref = region(turn(i, 1), 1)
            if ref is not None:
                sent.append(wire.copy(ref, ref, wire.left[axis]))
            self.fars.append(sent)
            if phase == 2:
                self.forward(region(turn(i, 3), None))
                self.forward(region(turn(i, 1), None))

    def end(self, phase):
        for plan, sent in zip(self.plans, self.fars):
            axis, region = plan[phase]
            i = self.wire.index[axis]
            for h, made in enumerate(sent):
                made.wait_recv()
                if phase == 2:
                    self.forward(region(turn(i, 2), h))

    def finish(self):
        for made in self.partner:
            made.wait_recv()


SLOTS = 128
CONVED = INNER + 2 * STATE
DT_AT = CONVED
BLOCK = 512
HIGH = lax.Precision.HIGHEST


def sigmoid(v):
    return 1.0 / (1.0 + jnp.exp(-v))


def dot_t(left, right):
    return lax.dot_general(left, right, (((1,), (1,)), ((), ())), preferred_element_type=F32)


def t_dot(left, right):
    return lax.dot_general(left, right, (((0,), (0,)), ((), ())), preferred_element_type=F32)


def exact(left, right):
    return jnp.dot(left, right, preferred_element_type=F32, precision=HIGH)


def lanes(p, width=128):
    return pl.ds(pl.multiple_of(p * width, width), width)


GATE = 384
COUNTS = {"in": WIN // BLOCK, "out": INNER // GATE}


def weight_block(kind, k):
    if kind == "in":
        return slice(None), lanes(k, BLOCK)
    return lax.div(k, 2), pl.ds(2 * lax.rem(k, 2), 2)


class Weights:
    def __init__(self, hbm, held, out, sems):
        self.hbm, self.held, self.out, self.sems = hbm, held, out, sems

    def copy(self, k):
        at = weight_block("in", k)
        return pltpu.make_async_copy(self.hbm.at[at], self.held.at[at], self.sems.at[k])

    def start(self):
        @pl.loop(0, COUNTS["in"])
        def _(k):
            self.copy(k).start()

    def wait(self, k):
        self.copy(k).wait()

    def get(self, k):
        return self.held[weight_block("in", k)]

    def columns(self, k):
        return self.out[:, :, :, :, lanes(k, BLOCK)].reshape(INNER, BLOCK)

    def again(self, kind, k):
        if kind == "in":
            return self.get(k)
        return self.out[weight_block(kind, k)].reshape(GATE, WIDTH)

    def done(self, kind, k):
        pass


class Stream:
    def __init__(self, hbm, slots, sems):
        self.hbm, self.slots = dict(zip(("in", "out"), hbm)), dict(zip(("in", "out"), slots))
        self.sems = dict(zip(("in", "out"), sems))

    def copy(self, kind, k):
        slot = lax.rem(k, self.slots[kind].shape[0])
        return pltpu.make_async_copy(
            self.hbm[kind].at[weight_block(kind, k)], self.slots[kind].at[slot], self.sems[kind].at[slot]
        )

    def start(self):
        for kind in ("out", "in"):
            for k in range(self.slots[kind].shape[0]):
                self.copy(kind, jnp.int32(k)).start()

    def again(self, kind, k):
        self.copy(kind, k).wait()
        got = self.slots[kind][lax.rem(k, self.slots[kind].shape[0])]
        return got if kind == "in" else got.reshape(GATE, WIDTH)

    def done(self, kind, k):
        count = self.slots[kind].shape[0]

        @pl.when(k + count < COUNTS[kind])
        def _():
            self.copy(kind, k + count).start()


def conv_tile(u, taps, lag):
    total = taps[4:5] + taps[3:4] * u
    for j in (1, 2, 3):
        total = total + taps[3 - j : 4 - j] * (pltpu.roll(u, j, 0) * lag[:, j : j + 1])
    return total


def conv_back(d_cv, u, taps, lag):
    d_u = taps[3:4] * d_cv
    rows = [None] * 5
    rows[4] = jnp.sum(d_cv, axis=0, keepdims=True)
    rows[3] = jnp.sum(d_cv * u, axis=0, keepdims=True)
    for j in (1, 2, 3):
        kept = d_cv * lag[:, j : j + 1]
        rows[3 - j] = jnp.sum(kept * pltpu.roll(u, j, 0), axis=0, keepdims=True)
        d_u = d_u + taps[3 - j : 4 - j] * pltpu.roll(kept, SLOTS - j, 0)
    return d_u, rows


def silu_slope(v):
    s = sigmoid(v)
    return s * (1.0 + v * (1.0 - s))


def triangle(lower):
    t = lax.broadcasted_iota(jnp.int32, (SLOTS, SLOTS), 0)
    s = lax.broadcasted_iota(jnp.int32, (SLOTS, SLOTS), 1)
    return jnp.where((s <= t) if lower else (s >= t), 1.0, 0.0).astype(F32)


def lane_index():
    return lax.broadcasted_iota(jnp.int32, (SLOTS, SLOTS), 1)


class Layer:
    def __init__(self, layer, **refs):
        self.layer = layer
        self.__dict__.update(refs)

    def taps(self, at):
        return self.rows[self.layer, :, at]

    def gain_in(self):
        return self.rows[self.layer, 5:6, :WIDTH]

    def gain_gate(self, k, width):
        return self.rows[self.layer, 5:6, pl.ds(pl.multiple_of(WIDTH + k * width, 128), width)]

    def head_rows(self):
        return self.heads[self.layer]


def pair_row(row, k=0):
    first = lax.broadcasted_iota(jnp.int32, (1, 128), 1) < 64
    return jnp.where(first, row[:, 2 * k : 2 * k + 1], row[:, 2 * k + 1 : 2 * k + 2])


def step_sizes(m):
    pre = m.pa[:, DT_AT : DT_AT + 128] + m.head_rows()[0:1]
    step = jnp.maximum(pre, 0.0) + jnp.log1p(jnp.exp(-jnp.abs(pre)))
    rate = -jnp.exp(m.head_rows()[1:2])
    m.step[...] = step
    level = exact(triangle(True), step * rate)
    m.level[...] = level
    m.level_t[...] = level.T


def states(m):
    cv = m.cv[:, INNER:CONVED]
    act = cv * sigmoid(cv)
    low = act.astype(BF)
    m.state_in[...] = low[:, :STATE]
    m.state_out[...] = low[:, STATE:]
    m.inner[...] = dot_t(low[:, STATE:], low[:, :STATE])


def group_columns(m, g):
    shift = lax.rem(SLOTS - 8 * g, SLOTS)
    return (
        pltpu.roll(m.level[...], shift, 1),
        pltpu.roll(m.step[...], shift, 1),
        m.level_t[pl.ds(pl.multiple_of(8 * g, 8), 8), :],
        pltpu.roll(m.head_rows(), shift, 1)[2:3],
    )


def pair_columns(m, p):
    shift = lax.rem(SLOTS - 2 * p, SLOTS)
    rows = [m.level_t[pl.ds(2 * p + e, 1), :] for e in (0, 1)]
    return (
        pltpu.roll(m.level[...], shift, 1),
        pltpu.roll(m.step[...], shift, 1),
        rows,
        pair_row(pltpu.roll(m.head_rows(), shift, 1)[2:3]),
    )


def nothing():
    pass


def forward(m, weights, halfway=nothing, mixed=nothing, gated=nothing, turned=nothing):
    r = m.resid[...]
    scale = lax.rsqrt(jnp.sum(r * r, axis=1, keepdims=True) * (1.0 / WIDTH) + EPS_NORM)
    live = m.lag[:, 0:1]
    m.normed[...] = (r * scale * m.gain_in()).astype(BF) * live.astype(BF)

    @pl.loop(0, WA // BLOCK)
    def _(k):
        weights.wait(k)
        m.pa[:, lanes(k, BLOCK)] = dot(m.normed[...], weights.get(k))

    step_sizes(m)
    lag = m.lag[...]
    m.cv[:, INNER:CONVED] = conv_tile(m.pa[:, INNER:CONVED], m.taps(slice(INNER, CONVED)), lag)
    states(m)

    @pl.loop(0, INNER // BLOCK)
    def _(k):
        weights.wait(WA // BLOCK + k)
        m.px[:, lanes(k, BLOCK)] = dot(m.normed[...], weights.get(WA // BLOCK + k))

    m.square[...] = jnp.zeros((SLOTS, 128), F32)

    def heads(g):
        level, step, rows, skips = group_columns(m, g)
        first = lane_index() < 64
        for k in range(4):
            at = lanes(4 * g + k)
            cv = conv_tile(m.px[:, at], m.taps(at), m.lag[...])
            m.cv[:, at] = cv
            act = cv * sigmoid(cv)
            both = jnp.where(first, step[:, 2 * k : 2 * k + 1], step[:, 2 * k + 1 : 2 * k + 2])
            scaled = act * both
            mixes = []
            for h in (2 * k, 2 * k + 1):
                decay = jnp.exp(level[:, h : h + 1] - rows[h : h + 1] + m.mask[...])
                mixes.append((m.inner[...] * decay).astype(BF))
            right = jnp.concatenate(
                [jnp.where(first, scaled, 0.0).astype(BF), jnp.where(first, 0.0, scaled).astype(BF)], axis=0
            )
            y = dot(jnp.concatenate(mixes, axis=1), right) + act * pair_row(skips, k)
            m.y[:, at] = y
            z = m.pa[:, at]
            gated = y * (z * sigmoid(z))
            m.work[:, at] = gated
            m.square[...] += gated * gated

    pl.loop(0, 3)(heads)
    halfway()
    pl.loop(3, 6)(heads)
    mixed()
    scale = lax.rsqrt(jnp.sum(m.square[...], axis=1, keepdims=True) * (1.0 / INNER) + EPS_NORM)
    m.gate_scale[...] = jnp.broadcast_to(scale, (SLOTS, 128))

    @pl.loop(0, INNER // BLOCK)
    def _(k):
        at = lanes(k, BLOCK)
        m.gate_low[:, at] = (m.work[:, at] * m.gate_scale[:, 0:1] * m.gain_gate(k, BLOCK)).astype(BF)

    gated()
    transposes(m)
    turned()

    @pl.loop(0, WIDTH // BLOCK)
    def _(k):
        at = lanes(k, BLOCK)
        branch = dot(m.gate_low[...], weights.columns(k))
        m.resid_out[:, at] = m.resid[:, at] + m.lag[:, 0:1] * branch


def transposes(m):
    @pl.loop(0, WIDTH // 128)
    def _(k):
        m.normed_t[lanes(k), :] = m.normed[:, lanes(k)].T

    @pl.loop(0, INNER // 128)
    def _(k):
        m.gate_t[lanes(k), :] = m.gate_low[:, lanes(k)].T


def branch_grad(m):
    m.d_c[...] = (m.upstream[...] * m.lag[:, 0:1]).astype(BF)


def backward(m, weights):
    m.square[...] = jnp.zeros((SLOTS, 128), F32)

    @pl.loop(0, COUNTS["out"])
    def _(k):
        at = lanes(k, GATE)
        d_gate = dot_t(m.d_c[...], weights.again("out", k))
        weights.done("out", k)
        m.work[:, at] = d_gate
        z = m.pa[:, at]
        hat = m.y[:, at] * (z * sigmoid(z)) * m.gate_scale[:, 0:1]
        m.grad_rows[5:6, pl.ds(pl.multiple_of(WIDTH + k * GATE, 128), GATE)] = jnp.sum(
            d_gate * hat, axis=0, keepdims=True
        )
        both = d_gate * m.gain_gate(k, GATE) * hat
        m.square[...] += both[:, :128] + both[:, 128:256] + both[:, 256:]

    m.square[...] = jnp.broadcast_to(
        jnp.sum(m.square[...], axis=1, keepdims=True) * (1.0 / INNER), (SLOTS, 128)
    )
    m.grad_heads[...] = jnp.zeros((8, 128), F32)
    m.d_inner[...] = jnp.zeros((SLOTS, 128), F32)
    m.d_level[...] = jnp.zeros((SLOTS, 128), F32)
    m.d_level_t[...] = jnp.zeros((SLOTS, 128), F32)
    m.d_step[...] = jnp.zeros((SLOTS, 128), F32)

    yield

    def heads(p):
        level, step, rows, skip = pair_columns(m, p)
        index = lane_index()
        first = index < 64
        at = lanes(p)
        z = m.pa[:, at]
        s = sigmoid(z)
        z_gate = z * s
        y = m.y[:, at]
        scale = m.gate_scale[...]
        hat = y * z_gate * scale
        d_gated = scale * (m.work[:, at] * m.gain_gate(p, 128) - hat * m.square[...])
        d_y = d_gated * z_gate
        d_z = d_gated * y * (s * (1.0 + z * (1.0 - s)))
        m.d_in[:, at] = d_z.astype(BF)
        cv = m.cv[:, at]
        s = sigmoid(cv)
        act = cv * s
        both = jnp.where(first, step[:, 0:1], step[:, 1:2])
        scaled = (act * both).astype(BF)
        d_ssd = jnp.concatenate(
            [jnp.where(first, d_y, 0.0).astype(BF), jnp.where(first, 0.0, d_y).astype(BF)], axis=0
        )
        d_mix = dot_t(d_ssd, scaled)
        mixes, sums = [], []
        for e in (0, 1):
            decay = jnp.exp(level[:, e : e + 1] - rows[e] + m.mask[...])
            mix = m.inner[...] * decay
            mixes.append(mix.astype(BF))
            one = d_mix[SLOTS * e : SLOTS * (e + 1)]
            m.d_inner[...] += one * decay
            gap = one * mix
            sums.append(jnp.sum(gap, axis=1, keepdims=True))
            m.d_level_t[pl.ds(2 * p + e, 1), :] = jnp.sum(gap, axis=0, keepdims=True)
        m.d_level[...] = jnp.where(index == 2 * p, sums[0], jnp.where(index == 2 * p + 1, sums[1], m.d_level[...]))
        d_scaled = t_dot(jnp.concatenate(mixes, axis=0), d_ssd)
        back = d_scaled * act
        one = jnp.sum(jnp.where(first, back, 0.0), axis=1, keepdims=True)
        two = jnp.sum(jnp.where(first, 0.0, back), axis=1, keepdims=True)
        m.d_step[...] = jnp.where(index == 2 * p, one, jnp.where(index == 2 * p + 1, two, m.d_step[...]))
        row = jnp.sum(d_y * act, axis=0, keepdims=True)
        one = jnp.sum(jnp.where(first[:1], row, 0.0), axis=1, keepdims=True)
        two = jnp.sum(jnp.where(first[:1], 0.0, row), axis=1, keepdims=True)
        m.grad_heads[2:3] = jnp.where(
            index[:1] == 2 * p, one, jnp.where(index[:1] == 2 * p + 1, two, m.grad_heads[2:3])
        )
        d_cv = (d_scaled * both + d_y * skip) * (s * (1.0 + cv * (1.0 - s)))
        d_u, grads = conv_back(d_cv, m.px[:, at], m.taps(at), m.lag[...])
        m.d_in[:, lanes(WA // 128 + p)] = d_u.astype(BF)
        for n in range(5):
            m.grad_rows[n : n + 1, at] = grads[n]

    pl.loop(0, HEADS // 4)(heads)
    yield
    pl.loop(HEADS // 4, HEADS // 2)(heads)
    yield

    d_inner = m.d_inner[...].astype(BF)
    d_out = dot(d_inner, m.state_in[...])
    d_in = t_dot(d_inner, m.state_out[...])
    for n, d_state in enumerate((d_in, d_out)):
        at = slice(INNER + STATE * n, INNER + STATE * (n + 1))
        d_cv = d_state * silu_slope(m.cv[:, at])
        d_u, grads = conv_back(d_cv, m.pa[:, at], m.taps(at), m.lag[...])
        m.d_in[:, at] = d_u.astype(BF)
        for k in range(5):
            m.grad_rows[k : k + 1, at] = grads[k]

    rate = -jnp.exp(m.head_rows()[1:2])
    run = exact(triangle(False), m.d_level[...] - m.d_level_t[...].T)
    d_step = m.d_step[...] + run * rate
    pre = m.pa[:, DT_AT : DT_AT + 128] + m.head_rows()[0:1]
    d_dt = d_step * sigmoid(pre)
    m.d_in[:, DT_AT : DT_AT + 128] = d_dt.astype(BF)
    m.d_in[:, DT_AT + 128 : WA] = jnp.zeros((SLOTS, WA - DT_AT - 128), BF)
    m.grad_heads[0:1] = jnp.sum(d_dt, axis=0, keepdims=True)
    m.grad_heads[1:2] = jnp.sum(run * m.step[...], axis=0, keepdims=True) * rate

    yield
    m.d_normed[...] = jnp.zeros((SLOTS, WIDTH), F32)

    @pl.loop(0, COUNTS["in"])
    def _(k):
        m.d_normed[...] += dot_t(m.d_in[:, lanes(k, BLOCK)], weights.again("in", k))
        weights.done("in", k)

    yield
    d_normed = m.d_normed[...] * m.lag[:, 0:1]
    r = m.resid[...].astype(F32)
    scale = lax.rsqrt(jnp.sum(r * r, axis=1, keepdims=True) * (1.0 / WIDTH) + EPS_NORM)
    hat = r * scale
    m.grad_rows[5:6, :WIDTH] = jnp.sum(d_normed * hat, axis=0, keepdims=True)
    d_hat = d_normed * m.gain_in()
    mean = jnp.sum(d_hat * hat, axis=1, keepdims=True) * (1.0 / WIDTH)
    m.upstream_out[...] = m.upstream[...] + scale * (d_hat - hat * mean)
    share_small(m)


def device_of(d):
    f, y = divmod(d, 4)
    return f // 8, f // 2 % 4, f % 2, y


def share_small(m):
    lane = lax.broadcasted_iota(jnp.int32, (8, 128), 1)
    row = lax.broadcasted_iota(jnp.int32, (8, 128), 0)
    heads = m.grad_heads[...]
    last = jnp.where(
        row == 6,
        jnp.where(lane < 64, heads[0:1], pltpu.roll(heads, 64, 1)[2:3]),
        heads[1:2],
    )

    def window(start, size):
        block, off = divmod(start, 128)
        tile = m.grad_rows[:, 128 * block : 128 * (block + 1)]
        if off + size > 128:
            tile = jnp.where(lane >= off, tile, m.grad_rows[:, 128 * (block + 1) : 128 * (block + 2)])
        return tile

    for d in range(128):
        tile = jnp.where(row < 5, window(26 * d, 26), window(36 * d, 36))
        m.shares[device_of(d)] = jnp.where(row < 6, tile, last)


PARAMS = ("mask", "lag", "rows", "heads")
ROWS_SHAPE = (LAYERS, 8, 4608)
HEADS_SHAPE = (LAYERS, 8, 128)
KEPT = (("pa", (SLOTS, WA), F32), ("px", (SLOTS, INNER), F32), ("cv", (SLOTS, CONVED), F32),
        ("y", (SLOTS, INNER), F32), ("gate_scale", (SLOTS, 128), F32))
OPERANDS = (("normed_t", (WIDTH, SLOTS), BF), ("gate_t", (INNER, SLOTS), BF))
RESULT = (("resid_out", (SLOTS, WIDTH), F32),)
GRADS = (("upstream_out", (SLOTS, WIDTH), F32), ("d_in", (SLOTS, WIN), BF), ("d_c", (SLOTS, WIDTH), BF), ("shares", (4, 4, 2, 4, 8, 128), F32))
SMALL = tuple((name, (SLOTS, 128), F32) for name in ("step", "level", "level_t", "inner", "square"))
STATES = (("state_in", (SLOTS, 128), BF), ("state_out", (SLOTS, 128), BF))
WORK = (("work", (SLOTS, INNER), F32),)
LOW = (("normed", (SLOTS, WIDTH), BF), ("gate_low", (SLOTS, INNER), BF))
BACK = tuple((name, (SLOTS, 128), F32) for name in ("d_inner", "d_level", "d_level_t", "d_step")) + (
    ("d_normed", (SLOTS, WIDTH), F32),
    ("grad_rows", (8, 4608), F32),
    ("grad_heads", (8, 128), F32),
)


class Phase:
    def __init__(self, wire, axis, half, tiles, index, term, refs):
        self.wire, self.axis, self.i = wire, axis, wire.index[axis]
        self.half, self.tiles, self.index, self.term = half, tiles, index, term
        self.opp, self.mid, self.from_left, self.from_right, self.acc = refs
        self.kind = self.opp.dtype

    def each(self, h, body):
        count = self.tiles[h]
        if count <= 2:
            for t in range(count):
                body(self.index(h, t), t)
        else:

            @pl.loop(0, count)
            def _(t):
                body(self.index(h, t), t)

    def device(self, h):
        return (self.wire.right if h == 0 else self.wire.left)[self.axis]

    def start(self):
        j = turn(self.i, 2)
        self.mids = [None, None]
        for h in (0, 1):
            if self.tiles[h]:

                def body(at, t, h=h):
                    self.opp[at] = self.term(j, h, t).astype(self.kind)

                self.each(h, body)
                part = self.half(h)
                self.mids[h] = self.wire.copy(self.opp.at[part], self.mid.at[part], self.device(h))

    def near(self):
        self.nears = []
        for h in (0, 1):
            if self.tiles[h]:
                self.mids[h].wait_recv()
                j = turn(self.i, 1 if h == 0 else 3)

                def body(at, t, h=h, j=j):
                    self.mid[at] = (self.term(j, h, t) + self.mid[at].astype(F32)).astype(self.kind)

                self.each(h, body)
                part = self.half(h)
                land = self.from_left if h == 0 else self.from_right
                self.nears.append(self.wire.copy(self.mid.at[part], land.at[part], self.device(h)))

    def alone(self):
        for h in (0, 1):
            if self.tiles[h]:
                self.wire.sent(self.mids[h])
                j = turn(self.i, 3 if h == 0 else 1)

                def body(at, t, h=h, j=j):
                    self.opp[at] = self.term(j, h, t).astype(self.kind)

                self.each(h, body)
                part = self.half(h)
                land = self.from_right if h == 0 else self.from_left
                self.nears.append(self.wire.copy(self.opp.at[part], land.at[part], self.device(1 - h)))

    def end(self):
        for made in self.nears:
            made.wait_recv()
        for h in (0, 1):

            def body(at, t, h=h):
                total = self.term(self.i, h, t) + self.from_left[at].astype(F32) + self.from_right[at].astype(F32)
                self.acc[at] = total.astype(self.acc.dtype)

            self.each(h, body)


def slab_shapes(part):
    if part is None:
        return ((4, 4, 8, 128), (4, 8, 128), (8, 128))
    kind, _, width, first = part
    rows, quarter = BLOCK_ROWS[kind], width // 4
    if first == "x":
        return ((4, rows, width), (rows, width), (rows, quarter))
    if first == "z":
        return ((4, rows, width), (4, rows, quarter), (rows, quarter))
    return ((4, 4, rows, quarter), (4, rows, quarter), (rows, quarter))


def pair(h):
    return pl.ds(2 * h, 2)


def part_phases(wire, part, left, right, bufs):
    kind, base, width, first = part
    rows, quarter = BLOCK_ROWS[kind], width // 4
    accs = [item[4] for item in bufs]
    every = slice(None)
    tile = 512 if kind == "in" else 256
    cut = block_half(rows, quarter)

    def block(h):
        (row, count), (col, size) = cut(h)
        return pl.ds(row, count), pl.ds(col, size)

    last_axis = {"x": "y", "z": "x", "y": "z"}[first]

    def last_term(j, h, t):
        at = block(h)
        if first == "x":
            (row, count), (col, size) = cut(h)
            return accs[1][pl.ds(row, count), cols(0, j, quarter, col, size)]
        return accs[1][j, at[0], at[1]]

    last = Phase(wire, last_axis, block, (1, 1), lambda h, t: block(h), last_term, bufs[2])
    if first in "xz":
        step = lambda t: pl.multiple_of(t * tile, tile)

        def one_term(j, h, t):
            lhs = left[j, pair(h)] if first == "x" else left[pair(h), j]
            rhs = right[:, pl.ds(pl.multiple_of(base + t * tile, tile), tile)]
            return dot(lhs.reshape(2 * rows, 256), rhs).reshape(2, rows, tile)

        one = Phase(
            wire, first, lambda h: (pair(h),), (width // tile,) * 2,
            lambda h, t: (pair(h), every, pl.ds(step(t), tile)), one_term, bufs[0],
        )
    else:

        def one_term(j, h, t):
            lhs = left[2 * h + lax.div(t, 2), pl.ds(2 * lax.rem(t, 2), 2)]
            return dot(lhs.reshape(2 * rows, 256), right[:, cols(base, j, quarter)]).reshape(2, rows, quarter)

        one = Phase(
            wire, "y", lambda h: (pair(h),), (4, 4),
            lambda h, t: (2 * h + lax.div(t, 2), pl.ds(2 * lax.rem(t, 2), 2)), one_term, bufs[0],
        )
    if first == "x":
        half = width // 2
        count = 1 if half < 1024 else 2
        size = half // count
        two = Phase(
            wire, "z", lambda h: (every, pl.ds(half * h, half)), (count, count),
            lambda h, t: (every, pl.ds(half * h + size * t, size)),
            lambda j, h, t: accs[0][j, :, pl.ds(half * h + size * t, size)].astype(F32), bufs[1],
        )
    elif first == "z":
        two = Phase(
            wire, "y", lambda h: (pair(h),), (2, 2), lambda h, t: (2 * h + t,),
            lambda j, h, t: accs[0][2 * h + t, :, cols(0, j, quarter)].astype(F32), bufs[1],
        )
    else:
        two = Phase(
            wire, "x", lambda h: (pair(h),), (2, 2), lambda h, t: (2 * h + t,),
            lambda j, h, t: accs[0][j, 2 * h + t].astype(F32), bufs[1],
        )
    return one, two, last


def small_phases(wire, own, far, bufs):
    accs = [item[4] for item in bufs]
    rows = lambda h: (pair(h),)
    at = lambda h, t: (2 * h + t,)
    return (
        Phase(wire, "y", rows, (2, 2), at, lambda j, h, t: own[2 * h + t, :, j] + far[2 * h + t, :, j], bufs[0]),
        Phase(wire, "x", rows, (2, 2), at, lambda j, h, t: accs[0][j, 2 * h + t], bufs[1]),
        Phase(
            wire, "z", lambda h: (pl.ds(0, 8),), (1, 0), lambda h, t: (pl.ds(0, 8),),
            lambda j, h, t: accs[1][j], bufs[2],
        ),
    )


class Reduce:
    def __init__(self, wire, parts, phases, pads, outs, picks):
        self.wire, self.parts, self.phases = wire, parts, phases
        self.pads, self.outs, self.picks, self.arrived = pads, outs, picks, []

    def start(self):
        for phases in self.phases:
            phases[0].start()

    def near(self, step):
        for phases in self.phases:
            phases[step].near()
        for phases in self.phases:
            phases[step].alone()

    def turn(self, step):
        for phases in self.phases:
            phases[step].end()
            phases[step + 1].start()

    def scatter(self):
        wire, y = self.wire, self.wire.y
        for part, phases, pad, out in zip(self.parts, self.phases, self.pads, self.outs):
            phases[2].end()
            if part is None:
                out[...] = phases[2].acc[...]
                continue
            low = phases[2].acc[...].astype(BF)
            pad[...] = dot(self.picks[part[0]][...], low).astype(BF).reshape(pad.shape)
            self.arrived += [
                wire.copy(pad.at[turn(y, by)], out.at[y], device_at(wire.x, wire.z, wire.core, turn(y, by)))
                for by in (1, 3, 2)
            ]
            out[y] = pad[y]

    def finish(self):
        for made in self.arrived:
            made.wait_recv()


def sum_shapes(parts):
    return [
        jax.ShapeDtypeStruct((4, PADDED[part[0]], part[2] // 4), BF) if part else jax.ShapeDtypeStruct((8, 128), F32)
        for part in parts
    ]


def ring_scratch(parts):
    scratch = []
    for part in parts:
        low = BF if part else F32
        for n, shape in enumerate(slab_shapes(part)):
            scratch += [pltpu.VMEM(shape, low)] * 4 + [pltpu.VMEM(shape, F32 if n else low)]
    return scratch + [pltpu.VMEM(shape.shape, shape.dtype) for shape in sum_shapes(parts)]


def take_ring(take, parts):
    return [[take(5) for _ in range(3)] for _ in parts], take(len(parts))


class Swap:
    def __init__(self, wire, src, dst, far_src, far_dst, sem):
        self.here = pltpu.make_async_copy(src, dst, sem)
        self.here.start()
        self.there = wire.copy(far_src, far_dst, wire.partner)

    def wait(self):
        self.here.wait()
        self.there.wait_recv()


def swap_rows(wire, ref, both, sem):
    c = wire.core
    return Swap(
        wire, ref.at[:, :, c], both.at[:, :, :, pl.ds(0, 128)],
        ref.at[:, :, 1 - c], both.at[:, :, :, pl.ds(128, 128)], sem,
    )


def swap_tokens(wire, ref, both, sem):
    return Swap(wire, ref, both.at[pl.ds(0, 128), :], ref, both.at[pl.ds(128, 128), :], sem)


IN_PARTS, OUT_PARTS = PARTS[:3], PARTS[3:]
BOTH = {"in": [(4, 4, 48, 256), (256, WIN)], "out": [(4, 4, 96, 256), (256, WIDTH)]}
PICKS = [(64, 48), (128, 96)]


def picks():
    return jnp.asarray(picker(12, 16).T, BF), jnp.asarray(picker(24, 32).T, BF)


def call_params(number):
    return pltpu.CompilerParams(collective_id=number, has_side_effects=True, vmem_limit_bytes=62 * 2**20)


def copies_of(parts):
    return sum(18 + 3 * (part is not None) for part in parts)


def sems(copies, local):
    return [pltpu.SemaphoreType.DMA((n,)) for n in (copies, copies, local)]


def last_layer(weights, params, inputs):
    ins = PARAMS + tuple(key for key, _ in inputs)
    outs = RESULT + OPERANDS + GRADS
    temps = KEPT + LOW + SMALL + STATES + WORK + BACK

    def kernel(*refs):
        refs = list(refs)
        take = lambda n: [refs.pop(0) for _ in range(n)]
        in_hbm, out_hbm = take(2)
        named = {key: refs.pop(0) for key in ins}
        named.update({entry[0]: refs.pop(0) for entry in outs + temps})
        held_in, held_out = take(2)
        block_sems, send, recv, local = take(4)
        wire = Wire(send, recv)
        m = Layer(LAYERS - 1, **named)
        moving = Weights(in_hbm, held_in, held_out, block_sems)
        moving.start()
        x, z, c, y = wire.x, wire.z, wire.core, wire.y
        plans = [gather_regions(part, held_out, x, z, c, y) for part in OUT_PARTS]
        sources = [gather_regions(part, out_hbm, x, z, c, y) for part in OUT_PARTS]
        placed = []
        for n, (plan, source) in enumerate(zip(plans, sources)):
            axis, region = plan[2]
            own = wire.index[axis]
            placed.append(pltpu.make_async_copy(source[2][1](own, None), region(own, None), local.at[n]))
            placed[n].start()
        wire.greet()
        for made in placed:
            made.wait()
        gather = Gather(wire, plans)
        gather.start(2)

        forward(
            m, moving, halfway=lambda: gather.middle(2), gated=lambda: gather.end(2), turned=gather.finish
        )
        branch_grad(m)
        for _ in backward(m, moving):
            pass
        wire.finish()

    made = pl.pallas_call(
        kernel,
        out_shape=[jax.ShapeDtypeStruct(shape, kind) for _, shape, kind in outs],
        in_specs=[ANY] * 2 + [VMEM] * len(ins),
        out_specs=[VMEM] * len(outs),
        scratch_shapes=[pltpu.VMEM(shape, kind) for _, shape, kind in temps]
        + [pltpu.VMEM((WIDTH, WIN), BF), pltpu.VMEM(MATRIX["out"], BF)]
        + [pltpu.SemaphoreType.DMA((COUNTS["in"],))]
        + sems(3 * 9, 3),
        compiler_params=call_params(3),
        name="forward_backward_last",
    )(*weights, *[params[key] for key in PARAMS], *[value for _, value in inputs])
    return {entry[0]: value for entry, value in zip(outs, made)}


SLOT_SHAPES = [(3, WIDTH, BLOCK), (3, 2, 2, 96, WIDTH)]
ALL_PARTS = PARTS + (None,)


def reduce_layer(name, number, grads, weights=(), params=None, inputs=()):
    ins = (PARAMS + tuple(key for key, _ in inputs)) if weights else ()
    results = GRADS if weights else ()
    temps = SMALL + STATES + WORK + BACK if weights else ()
    count = len(ALL_PARTS)

    def kernel(*refs):
        refs = list(refs)
        take = lambda n: [refs.pop(0) for _ in range(n)]
        p48, p96, n_in, d_in, g_in, dc_in, s_in = take(7)
        hbm = take(len(weights))
        named = {key: refs.pop(0) for key in ins}
        sums = take(count)
        named.update({entry[0]: refs.pop(0) for entry in results + temps})
        n2, d2, g2, dc2, s_own, s_far = take(6)
        bufs, pads = take_ring(take, ALL_PARTS)
        slots, slot_sems = (take(2), take(2)) if weights else ([], [])
        send, recv, local = take(3)
        wire = Wire(send, recv)
        c = wire.core
        if weights:
            m = Layer(0, **named)
            moving = Stream(hbm, slots, slot_sems)
            moving.start()
        wire.greet()
        swaps = [
            swap_rows(wire, g_in, g2, local.at[0]),
            swap_tokens(wire, dc_in, dc2, local.at[1]),
            swap_rows(wire, n_in, n2, local.at[2]),
            *[
                swap_tokens(wire, d_in.at[:, pl.ds(base, width)], d2.at[:, pl.ds(base, width)], local.at[n + 3])
                for n, (_, base, width, _) in enumerate(IN_PARTS)
            ],
            Swap(wire, s_in.at[:, :, c], s_own, s_in.at[:, :, 1 - c], s_far, local.at[6]),
        ]
        operands = {"in": (n2, d2), "out": (g2, dc2)}
        phases = [part_phases(wire, part, *operands[part[0]], bufs[n]) for n, part in enumerate(PARTS)]
        phases.append(small_phases(wire, s_own, s_far, bufs[count - 1]))
        choose = {"in": p48, "out": p96}
        cut = len(IN_PARTS)
        out = Reduce(wire, OUT_PARTS, phases[cut:-1], pads[cut:-1], sums[cut:-1], choose)
        rest = phases[:cut] + phases[-1:]
        rest = Reduce(
            wire, IN_PARTS + (None,), rest, pads[:cut] + pads[-1:], sums[:cut] + sums[-1:], choose
        )
        if weights:
            branch_grad(m)
            step_sizes(m)
            states(m)
        stages = backward(m, moving) if weights else iter(())
        for swap in swaps[:2]:
            swap.wait()
        out.start()
        swaps[2].wait()
        for swap, item in zip(swaps[3:6], phases):
            swap.wait()
            item[0].start()
        swaps[6].wait()
        phases[-1][0].start()
        next(stages, None)
        next(stages, None)
        out.near(0)
        rest.near(0)
        for _ in stages:
            pass
        out.turn(0)
        rest.turn(0)
        out.near(1)
        rest.near(1)
        out.turn(1)
        rest.turn(1)
        out.near(2)
        rest.near(2)
        out.scatter()
        rest.scatter()
        out.finish()
        rest.finish()
        wire.finish()

    out_shape = sum_shapes(ALL_PARTS)
    out_shape += [jax.ShapeDtypeStruct(shape, kind) for _, shape, kind in results]
    scratch = [pltpu.VMEM(shape, kind) for _, shape, kind in temps]
    scratch += [pltpu.VMEM(shape, BF) for shape in BOTH["in"] + BOTH["out"]]
    scratch += [pltpu.VMEM((4, 4, 4, 8, 128), F32)] * 2
    scratch += ring_scratch(ALL_PARTS)
    if weights:
        scratch += [pltpu.VMEM(shape, BF) for shape in SLOT_SHAPES]
        scratch += [pltpu.SemaphoreType.DMA((shape[0],)) for shape in SLOT_SHAPES]
    made = pl.pallas_call(
        kernel,
        out_shape=out_shape,
        in_specs=[VMEM] * 2 + [ANY] * (5 + len(weights)) + [VMEM] * len(ins),
        out_specs=[VMEM] * len(out_shape),
        scratch_shapes=scratch + sems(7 + copies_of(ALL_PARTS), 7),
        compiler_params=call_params(number),
        name=name,
    )(
        *picks(),
        grads["normed_t"].reshape(4, 4, 2, 48, 128),
        grads["d_in"],
        grads["gate_t"].reshape(4, 4, 2, 96, 128),
        grads["d_c"],
        grads["shares"],
        *weights,
        *([params[key] for key in PARAMS] if weights else []),
        *[value for _, value in inputs],
    )
    return made[:count], {entry[0]: value for entry, value in zip(results, made[count:])}


class Held:
    def __init__(self, refs):
        self.refs = refs

    def wait(self, k):
        pass

    def get(self, k):
        return self.refs["in"][:, :, :, :, lanes(k, BLOCK)].reshape(WIDTH, BLOCK)

    def columns(self, k):
        return self.refs["out"][:, :, :, :, lanes(k, BLOCK)].reshape(INNER, BLOCK)


def own_masks(lengths, owners, device, mask, lag):
    spots = lax.broadcasted_iota(jnp.int32, (1, 256), 1).astype(F32)
    length = lengths[...].astype(F32)
    hit = owners[...] == device
    earliest = jnp.min(jnp.where(hit, spots, 1e6), axis=1, keepdims=True)
    one = jnp.sum(jnp.where(hit & (spots == earliest), length, 0.0), axis=1, keepdims=True)
    two = jnp.sum(jnp.where(hit, length, 0.0), axis=1, keepdims=True)

    def segment(at):
        return jnp.where(at < one, 0.0, jnp.where(at < two, 1.0, 2.0))

    t = lax.broadcasted_iota(jnp.int32, (SLOTS, SLOTS), 0).astype(F32)
    s = lax.broadcasted_iota(jnp.int32, (SLOTS, SLOTS), 1).astype(F32)
    mask[...] = jnp.where((s <= t) & (segment(s) == segment(t)), 0.0, -1e30)
    same = jnp.where((t >= s) & (segment(t - s) == segment(t)), 1.0, 0.0)
    lag[...] = jnp.where(s == 0.0, jnp.where(t < two, 1.0, 0.0), same)


def small_tile(conv, gain, device):
    row = lax.broadcasted_iota(jnp.int32, (16, 128), 0)
    taps = jnp.zeros((16, 128), F32)
    norms = jnp.zeros((16, 128), F32)
    for layer in range(LAYERS):
        for k in range(5):
            line = jnp.pad(conv[k, layer : layer + 1, :], ((0, 0), (0, 102)))
            taps = jnp.where(row == 8 * layer + k, line, taps)
        line = jnp.pad(gain[layer : layer + 1, :], ((0, 0), (0, 92)))
        norms = jnp.where(row == 8 * layer + 5, line, norms)
    taps = pltpu.roll(taps, lax.rem(26 * device, 128), 1)
    norms = pltpu.roll(norms, lax.rem(36 * device, 128), 1)
    return jnp.where(lax.rem(row, 8) == 5, norms, taps).astype(BF)


def unpack_small(tiles, rows):
    lane = lax.broadcasted_iota(jnp.int32, (16, 128), 1)
    row = lax.rem(lax.broadcasted_iota(jnp.int32, (16, 128), 0), 8)

    def block(b, size):
        total = None
        for d in range(128):
            start, end = size * d - 128 * b, size * (d + 1) - 128 * b
            if end <= 0 or start >= 128:
                continue
            tile = tiles[device_of(d)].astype(F32)
            total = tile if total is None else jnp.where(lane >= start, tile, total)
        return total

    for b in range(36):
        total = block(b, 36)
        if b < 26:
            total = jnp.where(row == 5, total, block(b, 26))
        at = slice(128 * b, 128 * (b + 1))
        rows[0, :, at] = total[:8]
        rows[1, :, at] = total[8:]


def prepare_rows(refs, layer, row_in, ins):
    inner, state, step, out = refs
    row_in[...] = jnp.zeros(row_in.shape, F32)
    for r in range(12):
        at = slice(r, r + 1)
        row_in[at, :INNER] = inner[r, layer : layer + 1, :INNER]
        row_in[at, INNER:CONVED] = state[r, layer : layer + 1, :]
        row_in[at, DT_AT : DT_AT + HEADS] = step[r, layer : layer + 1, :]
        row_in[at, WA:] = inner[r, layer : layer + 1, INNER:]
    for (kind, base, width, _), ref in zip(PARTS, ins):
        for q in range(4):
            at = slice(base + q * width // 4, base + (q + 1) * width // 4)
            if kind == "in":
                ref[q] = row_in[:, at].astype(BF)
            else:
                cut = out[layer, :, at]
                ref[q] = jnp.concatenate([cut, jnp.zeros((8, width // 4), F32)], axis=0).astype(BF)


IN_SHAPES = [(4, PADDED[kind], width // 4) for kind, _, width, _ in PARTS]
OWN_SHAPES = [(BLOCK_ROWS[kind], width // 4) for kind, _, width, _ in PARTS]
GATHER_OUT = RESULT + KEPT + OPERANDS


def gather_kernel(*refs):
    refs = list(refs)
    take = lambda n: [refs.pop(0) for _ in range(n)]
    e48, e96 = take(2)
    matrices = take(4)
    conv, gain, head, tokens, lengths, owners = take(6)
    kept = dict(zip(MATRIX, take(2)))
    outs = dict(zip(MATRIX, take(2)))
    masks, lags, rows, heads = take(4)
    saved = take(len(GATHER_OUT))
    held = dict(zip(MATRIX, take(2)))
    temps = {entry[0]: refs.pop(0) for entry in GATHER_OUT + SMALL + STATES + WORK + LOW}
    (row_in,) = take(1)
    count = len(PARTS)
    ins = [take(count), take(count)]
    stages = [take(count), take(count)]
    owns = take(count)
    tiles, head_in, head_all, resid = take(4)
    send, recv, local = take(3)
    wire = Wire(send, recv)
    x, z, c, y = wire.x, wire.z, wire.core, wire.y
    device = (x * 8 + z * 2 + c) * 4 + y
    wire.greet()

    arrived = []
    def send_rows(layer):
        prepare_rows(matrices, layer, row_in, ins[layer])
        for n in range(count):
            stages[layer][n][y] = ins[layer][n][y]
            arrived.append(
                [
                    wire.copy(ins[layer][n].at[turn(y, by)], stages[layer][n].at[y], device_at(x, z, c, turn(y, by)))
                    for by in (1, 3, 2)
                ]
            )

    send_rows(0)
    send_rows(1)
    tiles[x, z, c, y] = small_tile(conv, gain, device)
    line = lax.broadcasted_iota(jnp.int32, (8, 128), 0)
    tile = jnp.zeros((8, 128), F32)
    for l in range(LAYERS):
        for j in range(3):
            part = jnp.pad(head[j, l : l + 1, :], ((0, 0), (0, 116)))
            tile = jnp.where(line == 3 * l + j, part, tile)
    tile = pltpu.roll(tile, 12 * y, 1)
    head_in[...] = tile
    head_all[y] = tile
    head_copies = [wire.copy(head_in, head_all.at[y], device_at(x, z, c, turn(y, by))) for by in (1, 3, 2)]

    def compact(layer, n):
        for made in arrived[count * layer + n]:
            made.wait_recv()
        got = stages[layer][n][...]
        flat = got.reshape(got.shape[0] * got.shape[1], got.shape[2])
        return dot((e96 if PARTS[n][0] == "out" else e48)[...], flat).astype(BF)

    for n, (kind, base, width, _) in enumerate(PARTS):
        held[kind][x, z, c, :, cols(base, y, width // 4)] = compact(0, n)

    plans = [
        [gather_regions(part, refs[part[0]], x, z, c, y) for part in PARTS] for refs in (held, outs)
    ]
    low = Gather(wire, plans[0] + [gather_regions(None, tiles, x, z, c, y)])
    top = Gather(wire, plans[1])
    top_in = Gather(wire, plans[1][: len(IN_PARTS)])
    low.start(0)
    placed = []
    for n, (kind, base, width, _) in enumerate(PARTS):
        owns[n][...] = compact(1, n)
        made = pltpu.make_async_copy(
            owns[n], outs[kind].at[x, z, c, :, cols(base, y, width // 4)], local.at[n]
        )
        made.start()
        placed.append(made)
    own_masks(lengths, owners, device, masks, lags)
    for made in head_copies:
        made.wait_recv()
    total = head_all[0] + head_all[1] + head_all[2] + head_all[3]
    for l in range(LAYERS):
        heads[l] = jnp.concatenate([total[3 * l : 3 * l + 3], jnp.zeros((5, 128), F32)], axis=0)
    resid[...] = tokens[...].astype(F32)
    for made in placed:
        made.wait()
    top.start(0)
    for phase in (0, 1):
        low.middle(phase)
        top.middle(phase)
        low.end(phase)
        low.start(phase + 1)
        top.end(phase)
        if phase == 0:
            top.start(1)
    low.middle(2)
    top_in.start(2)
    low.end(2)
    low.finish()
    stored = []
    for n, kind in enumerate(MATRIX):
        made = pltpu.make_async_copy(held[kind], kept[kind], local.at[count + n])
        made.start()
        stored.append(made)

    unpack_small(tiles, rows)
    m = Layer(0, resid=resid, mask=masks, lag=lags, rows=rows, heads=heads, **temps)
    forward(m, Held(held), mixed=lambda: top_in.middle(2))
    for n, entry in enumerate(GATHER_OUT):
        made = pltpu.make_async_copy(temps[entry[0]], saved[n], local.at[count + 2 + n])
        made.start()
        stored.append(made)
    top_in.end(2)
    top_in.finish()
    for made in stored:
        made.wait()
    wire.finish()


def gather_all(matrices, conv, gain, head, tokens, lengths, owners):
    copies = 2 * len(PARTS) * 3 + 3 + (2 * len(PARTS) + 1) * 18
    saved = GATHER_OUT
    temps = GATHER_OUT + SMALL + STATES + WORK + LOW
    out_shape = [jax.ShapeDtypeStruct(shape, BF) for shape in tuple(MATRIX.values()) * 2]
    out_shape += [
        jax.ShapeDtypeStruct(shape, F32)
        for shape in ((SLOTS, SLOTS), (SLOTS, SLOTS), ROWS_SHAPE, HEADS_SHAPE)
    ]
    out_shape += [jax.ShapeDtypeStruct(shape, kind) for _, shape, kind in saved]
    scratch = [pltpu.VMEM(shape, BF) for shape in MATRIX.values()]
    scratch += [pltpu.VMEM(shape, kind) for _, shape, kind in temps]
    scratch += [pltpu.VMEM((16, WIN), F32)]
    scratch += [pltpu.VMEM(shape, BF) for shape in IN_SHAPES * 4]
    scratch += [pltpu.VMEM(shape, BF) for shape in OWN_SHAPES]
    scratch += [
        pltpu.VMEM((4, 4, 2, 4, 16, 128), BF),
        pltpu.VMEM((8, 128), F32),
        pltpu.VMEM((4, 8, 128), F32),
        pltpu.VMEM((SLOTS, WIDTH), F32),
        pltpu.SemaphoreType.DMA((copies,)),
        pltpu.SemaphoreType.DMA((copies,)),
        pltpu.SemaphoreType.DMA((len(PARTS) + 2 + len(saved),)),
    ]
    made = pl.pallas_call(
        gather_kernel,
        out_shape=out_shape,
        in_specs=[VMEM] * 12,
        out_specs=[ANY] * 4 + [VMEM] * 4 + [ANY] * len(saved),
        scratch_shapes=scratch,
        compiler_params=pltpu.CompilerParams(
            collective_id=0, has_side_effects=True, vmem_limit_bytes=60 * 2**20
        ),
        name="gather_forward_first",
    )(
        jnp.asarray(picker(12, 16), BF),
        jnp.asarray(picker(24, 32), BF),
        *matrices, conv, gain, head, tokens, lengths, owners,
    )
    weights = [
        (w_in.reshape(WIDTH, WIN), w_out) for w_in, w_out in (made[:2], made[2:4])
    ]
    params = dict(zip(PARAMS, made[4:8]))
    return weights, params, {entry[0]: value for entry, value in zip(saved, made[8:])}


def adam(weight, moment, square, grad, rate, decay):
    moment = BETA_ONE * moment + (1.0 - BETA_ONE) * grad
    square = BETA_TWO * square + (1.0 - BETA_TWO) * grad * grad
    corr_one = 1.0 - BETA_ONE**STEP
    corr_two = 1.0 - BETA_TWO**STEP
    weight = weight - rate * (
        moment / corr_one / (jnp.sqrt(square / corr_two) + ADAM_EPS) + decay * weight
    )
    return (weight, moment, square)


RATES = ((RATE_MATRIX, WEIGHT_DECAY),) * 4 + ((RATE_VECTOR, 0.0),) * 2 + ((RATE_HEADS, 0.0),)


def update_kernel(count, *refs):
    refs = list(refs)
    take = lambda n: [refs.pop(0) for _ in range(n)]
    hbm, results, held = take(count), take(28), take(count)
    (arrive,) = take(1)
    fetched = [pltpu.make_async_copy(src, dst, arrive.at[n]) for n, (src, dst) in enumerate(zip(hbm, held))]
    for made in fetched:
        made.start()
    for made in fetched:
        made.wait()
    refs = held + results
    summed = [take(len(PARTS) + 1) for _ in range(LAYERS)]
    olds = [take(3) for _ in range(7)]
    news = [take(3) for _ in range(7)]
    inner, state, step, out, conv, gain, head = take(7)
    places = ((inner, 0, INNER, 0), (state, INNER, CONVED, 0), (step, DT_AT, DT_AT + HEADS, 0), (inner, WA, WIN, INNER))
    x, z, c, y = place()
    device = (x * 8 + z * 2 + c) * 4 + y
    for layer, (*sums, tile) in enumerate(summed):
        at = slice(layer, layer + 1)
        for (kind, base, width, _), cut in zip(PARTS, sums):
            size = width // 4
            for q in range(4):
                part = cut[q].astype(F32)
                start = base + q * size
                if kind == "out":
                    out[layer, :, start : start + size] = part[:24]
                    continue
                for ref, low, high, to in places:
                    first, last = max(low, start), min(high, start + size)
                    if first < last:
                        for r in range(12):
                            ref[r, at, to + first - low : to + last - low] = part[
                                r : r + 1, first - start : last - start
                            ]
        taps = pltpu.roll(tile[...], lax.rem(SLOTS * 32 - 26 * device, 128), 1)
        norms = pltpu.roll(tile[...], lax.rem(SLOTS * 64 - 36 * device, 128), 1)
        mine = pltpu.roll(tile[...], lax.rem(SLOTS - 12 * y, 128), 1)
        for k in range(5):
            conv[k, at, :] = taps[k : k + 1, :26]
        gain[at, :] = norms[5:6, :36]
        head[0, at, :] = mine[6:7, :12]
        head[1, at, :] = mine[7:8, :12]
        head[2, at, :] = mine[6:7, 64:76]

    for old, new, grad, (rate, decay) in zip(olds, news, (inner, state, step, out, conv, gain, head), RATES):

        def body(at, old=old, new=new, grad=grad, rate=rate, decay=decay):
            values = adam(old[0][at], old[1][at], old[2][at], grad[at], rate, decay)
            for ref, value in zip(new, values):
                ref[at] = value

        if grad.shape[0] == 12:

            @pl.loop(0, 12)
            def _(r, body=body):
                body(r)
        else:
            body(...)


def update_all(summed, olds):
    flat = [ref for item in summed for ref in item] + [ref for item in olds for ref in item]
    shapes = [jax.ShapeDtypeStruct(item[0].shape, F32) for item in olds]
    return pl.pallas_call(
        partial(update_kernel, len(flat)),
        out_shape=[shape for shape in shapes for _ in range(3)] + shapes,
        in_specs=[ANY] * len(flat),
        out_specs=[VMEM] * 28,
        scratch_shapes=[pltpu.VMEM(item.shape, item.dtype) for item in flat]
        + [pltpu.SemaphoreType.DMA((len(flat),))],
        compiler_params=pltpu.CompilerParams(vmem_limit_bytes=62 * 2**20),
        name="update",
    )(*flat)


def shards(
    tokens,
    cotangent,
    seq_lengths,
    seq_owner,
    inner_weight,
    inner_moment,
    inner_square,
    state_weight,
    state_moment,
    state_square,
    step_weight,
    step_moment,
    step_square,
    out_weight,
    out_moment,
    out_square,
    conv_weight,
    conv_moment,
    conv_square,
    gains,
    gain_moment,
    gain_square,
    head_params,
    head_moment,
    head_square,
):
    middle = lambda v: v.transpose(1, 0, 2)
    last = lambda v: v.transpose(2, 0, 1)
    same = lambda v: v
    views = (
        (middle, middle, (inner_weight, inner_moment, inner_square)),
        (middle, middle, (state_weight, state_moment, state_square)),
        (middle, middle, (step_weight, step_moment, step_square)),
        (same, same, (out_weight, out_moment, out_square)),
        (last, lambda v: v.transpose(1, 2, 0), (conv_weight, conv_moment, conv_square)),
        (same, same, (gains, gain_moment, gain_square)),
        (middle, middle, (head_params, head_moment, head_square)),
    )
    olds = [[view(item) for item in items] for view, _, items in views]
    firsts = [item[0] for item in olds]
    weights, params, low = gather_all(
        firsts[:4], firsts[4], firsts[5], firsts[6], tokens, seq_lengths.reshape(1, 256), seq_owner.reshape(1, 256)
    )
    top = last_layer(weights[1], params, [("resid", low["resid_out"]), ("upstream", cotangent)])
    below = [("resid", tokens), ("upstream", top["upstream_out"])] + [(key, low[key]) for key, _, _ in KEPT]
    sums_top, bottom = reduce_layer("reduce_last_backward_first", 1, top, weights[0], params, below)
    sums_low, _ = reduce_layer("reduce_first", 2, {**low, **bottom})
    made = update_all([sums_low, sums_top], olds)
    results = [top["resid_out"], bottom["upstream_out"]]
    for n, (_, back, _) in enumerate(views):
        results += [back(item) for item in made[3 * n : 3 * n + 3]]
    results += [back(item) for (_, back, _), item in zip(views, made[21:])]
    return tuple(results)


ROWS = P(("fsdp", "sub"), None)
SPLIT = P(None, ("fsdp", "sub"), None)
FLAT = P(None, ("fsdp", "sub"))
HEAD = P(None, None, "sub")


def solution(mesh):
    return jax.shard_map(
        shards,
        mesh=mesh,
        in_specs=(ROWS, ROWS, P(), P()) + (SPLIT,) * 15 + (FLAT,) * 3 + (HEAD,) * 3,
        out_specs=(ROWS, ROWS) + (SPLIT,) * 15 + (FLAT,) * 3 + (HEAD,) * 3 + (SPLIT,) * 5 + (FLAT, HEAD),
        check_vma=False,
    )
```
